256 devices in a mesh: grp: 16 (over z, core), sub: 16 (over y, x).
Axes of the slice: x: 4, y: 4, z: 8, core: 2. Of those that a mesh axis runs over, the one named last changes fastest.
Arguments:
- macro_state: float32 [1024, 256, 256], P('grp', 'sub'), may hold values from 0 to 6, as said below
- macro_sizes: int32 [1024], replicated, may hold values from 64 to 256
- block_sources: int32 [1024, 4], replicated, may hold values from 0 to 1023, as said below
- event_rates: float32 [1024, 4], P('grp'), may hold values from 0.1 to 1
- first_factor: float32 [4, 256, 256], replicated, may hold values from 0 to 0.015625
- first_pattern: int32 [4, 16, 16], replicated, may hold values 0 or 1
- second_factor: float32 [4, 256, 256], replicated, may hold values from 0 to 0.015625
- second_pattern: int32 [4, 16, 16], replicated, may hold values 0 or 1
Outputs:
- next_state: float32 [1024, 256, 256], P('grp', 'sub')
- growth: float32 [], replicated
The draws below stay inside these ranges and needn't reach their ends.
Inputs may be any that keep to these rules, and one draw needn't show every extreme that they name: `block_sources`: among the 256 blocks of the macro states of one group, at most 24 name source macro states of any one group, and in every group exactly 24 name some one group. `macro_state`: Positive.
All inputs are finite; a program needn't handle non-finite values.
Results may differ from the reference program's by a relative error of at most 0.00007.
Values sent between devices are 32-bit elements; how exact they have to be, the bound alone decides.
A program may use at most 64 MiB of HBM per device.

```python
import math
import jax
import jax.numpy as jnp
from jax import lax

NS = 256
NBLK = 16
EVENTS = 4
MAC_GRP = 64
MACROS = 1024


def widen_blocks(block_scale):
    block_size = NS // NBLK
    return jnp.repeat(jnp.repeat(block_scale, block_size, axis=1), block_size, axis=2)


def draw_macro_state(key, part):
    key = jax.random.fold_in(key, 5)
    key_macro = jax.random.fold_in(key, 0)
    key_cells = jax.random.fold_in(key, 2)
    key_blocks = jax.random.fold_in(key, 3)
    rising = 3.0 ** (jnp.arange(MACROS, dtype=jnp.float32) / MACROS)
    cells = jnp.exp(jax.random.uniform(key_cells, (MACROS, NS, NS), jnp.float32, math.log(0.001), 0.0))
    macro_scale = jnp.exp(jax.random.uniform(key_macro, (MACROS,), jnp.float32, math.log(0.5), math.log(2.0)))
    block_scale = jnp.exp(jax.random.uniform(key_blocks, (MACROS, NBLK, NBLK), jnp.float32, math.log(0.1), 0.0))
    values = (rising * macro_scale)[:, None, None] * widen_blocks(block_scale) * cells
    return values.astype(jnp.float32)


def draw_block_sources(key, part):
    key = jax.random.fold_in(key, 11)
    num_groups = MACROS // MAC_GRP
    per_group = EVENTS * MAC_GRP
    average = per_group // num_groups
    key_heavy, key_light, key_order, key_pick = jax.random.split(key, 4)
    position = jnp.arange(per_group, dtype=jnp.int32)
    labels = jnp.broadcast_to(position % num_groups, (num_groups, per_group))
    heavy = jax.random.randint(key_heavy, (num_groups,), 0, num_groups)
    light = (heavy + 1 + jax.random.randint(key_light, (num_groups,), 0, num_groups - 1)) % num_groups
    moved = (labels == light[:, None]) & ((position // num_groups)[None, :] < average // 2)
    labels = jnp.where(moved, heavy[:, None], labels)

    def shuffle(group_key):
        return jax.random.permutation(group_key, per_group)
    orders = jax.vmap(shuffle)(jax.random.split(key_order, num_groups))
    labels = jnp.take_along_axis(labels, orders, axis=1)
    offsets = jax.random.randint(key_pick, (num_groups, per_group), 0, MAC_GRP)
    return (labels * MAC_GRP + offsets).reshape(MACROS, EVENTS).astype(jnp.int32)


def plant(entries, stream_key, low, high):
    dims = entries.shape
    index_at = [jax.random.randint(jax.random.fold_in(stream_key, axis), (), 0, dims[axis]) for axis in range(len(dims))]
    entries = entries.at[tuple(index_at)].set(low)
    longest = dims.index(max(dims))
    index_at[longest] = (index_at[longest] + 1) % dims[longest]
    return entries.at[tuple(index_at)].set(high)


def level_of(stream_key, dims, cuts, smallest, top_value):
    gain, own = 1.0, jax.random.fold_in(stream_key, 6)
    for dim, shards_of in cuts:
        steps = jnp.exp(jax.random.uniform(jax.random.fold_in(own, dim), (shards_of,), jnp.float32, smallest / len(cuts), top_value / len(cuts)))
        gain = gain * jnp.repeat(steps, dims[dim] // shards_of).reshape([-1 if axis == dim else 1 for axis in range(len(dims))])
    return gain


def setup_inputs(seed: int = 0) -> dict:
    key_list = jax.random.split(jax.random.key(seed), 9)
    macro_state = draw_macro_state(jax.random.fold_in(key_list[8], 71), 0)
    macro_sizes = plant(jax.random.randint(key_list[1], (MACROS,), NS // 4, NS + 1), jax.random.fold_in(key_list[1], 1), NS // 4, NS).astype(jnp.int32)
    block_sources = draw_block_sources(jax.random.fold_in(key_list[8], 71), 0)
    event_rates = jnp.clip(jnp.exp(math.log(1.0) - 2.3025851 * jax.random.uniform(key_list[3], (MACROS, EVENTS), jnp.float32) ** level_of(key_list[3], (MACROS, EVENTS), ((0, 16),), -0.2, 0.2)), 0.1, 1.0)
    first_factor = jnp.clip(jax.random.uniform(key_list[4], (EVENTS, NS, NS), jnp.float32, 0.0, 0.015625), 0.0, 0.015625)
    first_pattern = plant((jax.random.randint(key_list[5], (EVENTS, NBLK, NBLK), 0, 2) < 1).astype(jnp.int32), jax.random.fold_in(key_list[5], 1), 0, 1)
    second_factor = jnp.clip(jax.random.uniform(key_list[6], (EVENTS, NS, NS), jnp.float32, 0.0, 0.015625), 0.0, 0.015625)
    second_pattern = plant((jax.random.randint(key_list[7], (EVENTS, NBLK, NBLK), 0, 2) < 1).astype(jnp.int32), jax.random.fold_in(key_list[7], 1), 0, 1)
    return dict(macro_state=macro_state, macro_sizes=macro_sizes, block_sources=block_sources, event_rates=event_rates, first_factor=first_factor, first_pattern=first_pattern, second_factor=second_factor, second_pattern=second_pattern)


highest = lax.Precision.HIGHEST


def expand(values, pattern):
    factor_blocks = pattern.shape[1]
    block_size = values.shape[1] // factor_blocks
    widened = jnp.repeat(jnp.repeat(pattern.astype(jnp.float32), block_size, axis=1), block_size, axis=2)
    return values * widened


def reference(macro_state, macro_sizes, block_sources, event_rates, first_factor, first_pattern, second_factor, second_pattern):
    first = expand(first_factor, first_pattern)
    second = expand(second_factor, second_pattern)
    macros, order, _ = macro_state.shape
    num_events = block_sources.shape[1]
    row_index = lax.iota(jnp.int32, order)
    alive = (row_index[None, :] < macro_sizes[:, None]).astype(jnp.float32)
    masked = macro_state * alive[:, :, None]
    batch_width = math.gcd(macros, 16)

    def apply_batch(inputs):
        batch_sources, batch_rates, batch_alive = inputs
        gathered = masked[batch_sources]
        scaled = jnp.einsum("mkrc,kdc->mkrd", gathered, second, precision=highest) * batch_rates[:, :, None, None]
        return jnp.einsum("kar,mkrc->mac", first, scaled, precision=highest) * batch_alive[:, :, None]

    product = lax.map(apply_batch, (block_sources.reshape(macros // batch_width, batch_width, num_events),
                                    event_rates.reshape(macros // batch_width, batch_width, num_events),
                                    alive.reshape(macros // batch_width, batch_width, order)))
    product = product.reshape(macros, order, order)
    total = jnp.sum(product)
    mass = jnp.sum(masked)
    live_count = order * jnp.sum(macro_sizes).astype(jnp.float32)
    return product * (live_count / total), total / mass
```

```python
import jax
import jax.numpy as jnp
from jax import lax
from jax.experimental import pallas as pl
from jax.experimental.pallas import tpu as pltpu
from jax.sharding import PartitionSpec as P

MESH = pl.DeviceIdType.MESH
F32, BF16 = jnp.float32, jnp.bfloat16
NS = 256
EVENTS = 4
NZ = 8
NSUB = 16
MAC = 64
OWN = MAC // NSUB
BLK = OWN * EVENTS
GROUPS = 2 * NZ
HALF = MAC // 2
CHUNKS = 4
CW, CCW = 0, 1


def split(x):
    high = x.astype(BF16)
    return high, (x - high.astype(F32)).astype(BF16)


def dot(a, b):
    return jnp.dot(a, b, preferred_element_type=F32)


def kernel(
    state_ref, sizes_ref, sizes_vec_ref, sources_ref, rates_ref, first_ref, fpat_ref, second_ref, spat_ref,
    out_ref, stats_ref,
    g0, g1, g2, g3, sb0, sb1, sb2, sb3, rb0, rb1, rb2, rb3,
    fh, fl, stc, zacc, zh, zl, pacc, pb, sums, tsub, tgrp,
    ring_send, ring_recv, d2d_send, d2d_recv, xy_send, xy_recv, tot_send, tot_recv, out_send, out_recv,
):
    gathered, outgo, income = (g0, g1, g2, g3), (sb0, sb1, sb2, sb3), (rb0, rb1, rb2, rb3)
    group, piece = lax.axis_index("grp"), lax.axis_index("sub")
    z, core = group // 2, group % 2
    y, x = piece // 4, piece % 4
    sibling = z * 2 + (1 - core)

    def ring_group(distance):
        return ((z + distance + NZ) % NZ) * 2 + core

    def sub_peer(offset):
        return ((y + offset // 4) % 4) * 4 + (x + offset % 4) % 4

    barrier = pltpu.get_barrier_semaphore()

    @pl.loop(1, NSUB)
    def _(offset):
        pl.semaphore_signal(barrier, inc=1, device_id=(group, sub_peer(offset)), device_id_type=MESH)

    @pl.loop(1, GROUPS)
    def _(offset):
        pl.semaphore_signal(barrier, inc=1, device_id=((group + offset) % GROUPS, piece), device_id_type=MESH)

    row_iota = lax.broadcasted_iota(jnp.int32, (8, 128), 0)

    def stage(q, mass):
        rh, ch = q // 2, q % 2
        rows = row_iota + (piece * 16 + rh * 8)

        def body(m, mass):
            tile = state_ref[m, pl.ds(8 * rh, 8), pl.ds(128 * ch, 128)]
            tile = jnp.where(rows < sizes_ref[group * MAC + m], tile, 0.0)
            gathered[q][group * MAC + m] = tile
            return mass + tile

        return lax.fori_loop(0, MAC, body, mass, unroll=8)

    def ring_piece(q, distance, h):
        return gathered[q].at[pl.ds(ring_group(distance) * MAC + HALF * h, HALF)]

    def ring_copy(q, way, t, h):
        sign = -1 if way == CW else 1
        part = ring_piece(q, sign * (t - 1), h)
        return pltpu.make_async_remote_copy(
            src_ref=part,
            dst_ref=part,
            send_sem=ring_send.at[q],
            recv_sem=ring_recv.at[((q * 2 + way) * 4 + t - 1) * 2 + h],
            device_id=(ring_group(-sign), piece),
            device_id_type=MESH,
        )

    def ring_wait(q, way, t, h):
        sign = -1 if way == CW else 1
        part = ring_piece(q, sign * t, h)
        pltpu.make_async_copy(part, part, ring_recv.at[((q * 2 + way) * 4 + t - 1) * 2 + h]).wait()

    def sibling_copy(q, part):
        pltpu.make_async_remote_copy(
            src_ref=part,
            dst_ref=part,
            send_sem=d2d_send.at[q],
            recv_sem=d2d_recv.at[q],
            device_id=(sibling, piece),
            device_id_type=MESH,
        ).start()

    def carried(way, t):
        return (0, 1) if t < 4 else ((0,) if way == CW else (1,))

    def ring_start(q):
        for h in (0, 1):
            for way in (CW, CCW):
                ring_copy(q, way, 1, h).start()
        sibling_copy(q, gathered[q].at[pl.ds(group * MAC, MAC)])

    def ring_step(q, t):
        for h in (0, 1):
            for way in (CW, CCW):
                if h in carried(way, t):
                    ring_wait(q, way, t, h)
                    if t < 4 and h in carried(way, t + 1):
                        ring_copy(q, way, t + 1, h).start()
                    sibling_copy(q, ring_piece(q, -t if way == CW else t, h))

    def prepare(k):
        rows_of = (lax.broadcasted_iota(jnp.int32, (NS, 16), 0) // 16 == lax.broadcasted_iota(jnp.int32, (NS, 16), 1))
        cols_of = (lax.broadcasted_iota(jnp.int32, (16, NS), 1) // 16 == lax.broadcasted_iota(jnp.int32, (16, NS), 0))
        rows_of, cols_of = rows_of.astype(F32).astype(BF16), cols_of.astype(F32).astype(BF16)

        def widen(pattern):
            return dot(dot(rows_of, pattern.astype(F32).astype(BF16)).astype(BF16), cols_of)

        source = lax.broadcasted_iota(jnp.int32, (NS, NS), 0)
        target = lax.broadcasted_iota(jnp.int32, (NS, NS), 1)
        place = (source // 8 % 2) * 128 + (source // 16) * 8 + source % 8
        order = (place == target).astype(F32).astype(BF16)
        high, low = split(first_ref[k] * widen(fpat_ref[k]))
        for part, dest in ((high, fh), (low, fl)):
            moved = dot(part, order).astype(BF16)
            for rh in (0, 1):
                dest[rh, :, k * 128 : (k + 1) * 128] = moved[:, rh * 128 : (rh + 1) * 128]
        high, low = split((second_ref[k] * widen(spat_ref[k])).T)
        for ch in (0, 1):
            rows = slice(ch * 128, ch * 128 + 128)
            stc[k, ch, 0:128, :] = high[rows]
            stc[k, ch, 128:256, :] = low[rows]
            stc[k, ch, 256:384, :] = high[rows]

    def select(q):
        pltpu.make_async_copy(
            gathered[q].at[pl.ds(0, 512)], gathered[q].at[pl.ds(0, 512)], d2d_recv.at[q]
        ).wait()

        def pick(j, dest, at):
            tiles = [
                gathered[q][sources_ref[k, group * MAC + j * OWN + mm]] for k in range(EVENTS) for mm in range(OWN)
            ]
            for b, tile in enumerate(tiles):
                dest[at, b] = tile

        @pl.loop(1, NSUB)
        def _(offset):
            j = sub_peer(offset)
            pick(j, outgo[q], j)
            pltpu.make_async_remote_copy(
                src_ref=outgo[q].at[j],
                dst_ref=income[q].at[piece],
                send_sem=xy_send.at[q],
                recv_sem=xy_recv.at[q],
                device_id=(group, j),
                device_id_type=MESH,
            ).start()

        pick(piece, income[q], piece)

    def stage1(q):
        rh, ch = q // 2, q % 2
        pltpu.make_async_copy(
            income[q].at[pl.ds(0, NSUB - 1)], income[q].at[pl.ds(0, NSUB - 1)], xy_recv.at[q]
        ).wait()
        for k in range(EVENTS):
            block = income[q][:, k * OWN : (k + 1) * OWN].reshape(NSUB * OWN * 8, 128)
            high, low = split(block)
            part = dot(jnp.concatenate([high, high, low], axis=1), stc[k, ch])
            if ch == 0:
                zacc[k] = part
            else:
                part = (part + zacc[k]).reshape(NSUB, OWN, 8, NS)
                for mm in range(OWN):
                    rate = rates_ref[k, piece * OWN + mm]
                    high, low = split(part[:, mm].reshape(128, NS) * rate)
                    zh[mm, k * 128 : (k + 1) * 128, :] = high
                    zl[mm, k * 128 : (k + 1) * 128, :] = low

    def stage2(mm, rh):
        high, low = zh[mm], zl[mm]
        return dot(fh[rh], high) + dot(fh[rh], low) + dot(fl[rh], high)

    mass = stage(0, jnp.zeros((8, 128), F32))
    pl.semaphore_wait(barrier, NSUB - 1 + GROUPS - 1)
    ring_start(0)
    for q in range(1, CHUNKS):
        mass = stage(q, mass)
    sums[1] = mass

    for q in range(CHUNKS):
        for t in range(1, 5):
            ring_step(q, t)
            if t == 3 and q + 1 < CHUNKS:
                ring_start(q + 1)
            if q == 0:
                prepare(t - 1)
            if q > 0 and t == 1:
                select(q - 1)
            if q > 0 and t == 4:
                if q < CHUNKS - 1:
                    stage1(q - 1)
                if q == 2:
                    for mm in range(OWN):
                        pacc[mm] = stage2(mm, 0)

    select(CHUNKS - 1)
    stage1(CHUNKS - 2)
    stage1(CHUNKS - 1)

    all_rows = lax.broadcasted_iota(jnp.int32, (NS, NS), 0)
    total = jnp.zeros((8, NS), F32)
    for mm in range(OWN):
        size = sizes_ref[group * MAC + piece * OWN + mm]
        product = jnp.where(all_rows < size, pacc[mm] + stage2(mm, 1), 0.0)
        total = total + jnp.sum(product.reshape(NS // 8, 8, NS), axis=0)
        pb[:, mm] = product.reshape(NSUB, 16, NS)
    sums[0] = total[:, :128] + total[:, 128:]

    tsub[piece] = sums[...]

    @pl.loop(1, NSUB)
    def _(offset):
        pltpu.make_async_remote_copy(
            src_ref=sums,
            dst_ref=tsub.at[piece],
            send_sem=tot_send.at[0],
            recv_sem=tot_recv.at[0],
            device_id=(group, sub_peer(offset)),
            device_id_type=MESH,
        ).start()

    @pl.loop(1, NSUB)
    def _(offset):
        j = sub_peer(offset)
        pltpu.make_async_remote_copy(
            src_ref=pb.at[j],
            dst_ref=out_ref.at[piece],
            send_sem=out_send,
            recv_sem=out_recv,
            device_id=(group, j),
            device_id_type=MESH,
        ).start()

    out_ref[piece] = pb[piece]
    pltpu.make_async_copy(tsub.at[pl.ds(0, NSUB - 1)], tsub.at[pl.ds(0, NSUB - 1)], tot_recv.at[0]).wait()
    tgrp[group] = jnp.sum(tsub[...], axis=0)

    @pl.loop(1, GROUPS)
    def _(offset):
        pltpu.make_async_remote_copy(
            src_ref=tgrp.at[group],
            dst_ref=tgrp.at[group],
            send_sem=tot_send.at[1],
            recv_sem=tot_recv.at[1],
            device_id=((group + offset) % GROUPS, piece),
            device_id_type=MESH,
        ).start()

    for q in range(CHUNKS):
        part = gathered[q].at[pl.ds(0, 14 * HALF)]
        pltpu.make_async_copy(part, part, ring_send.at[q]).wait()
        part = gathered[q].at[pl.ds(0, MAC + 14 * HALF)]
        pltpu.make_async_copy(part, part, d2d_send.at[q]).wait()
        part = outgo[q].at[pl.ds(0, NSUB - 1)]
        pltpu.make_async_copy(part, part, xy_send.at[q]).wait()
    part = tsub.at[pl.ds(0, NSUB - 1)]
    pltpu.make_async_copy(part, part, tot_send.at[0]).wait()
    live = jnp.sum(sizes_vec_ref[...].astype(F32)) * NS

    part = tgrp.at[pl.ds(0, GROUPS - 1)]
    pltpu.make_async_copy(part, part, tot_recv.at[1]).wait()
    both = jnp.sum(tgrp[...], axis=0)
    total, mass = jnp.sum(both[0]), jnp.sum(both[1])
    pick = lax.broadcasted_iota(jnp.int32, (8, 128), 0) == 0
    numer = jnp.where(pick, jnp.full((8, 128), live, F32), jnp.full((8, 128), total, F32))
    denom = jnp.where(pick, jnp.full((8, 128), total, F32), jnp.full((8, 128), mass, F32))
    stats_ref[...] = numer / denom

    pltpu.make_async_copy(part, part, tot_send.at[1]).wait()
    part = pb.at[pl.ds(0, NSUB - 1)]
    pltpu.make_async_copy(part, part, out_recv).wait()
    pltpu.make_async_copy(part, part, out_send).wait()


def on_device(
    macro_state, macro_sizes, block_sources, event_rates, first_factor, first_pattern, second_factor, second_pattern
):
    vmem, smem = pl.BlockSpec(memory_space=pltpu.VMEM), pl.BlockSpec(memory_space=pltpu.SMEM)
    dma = pltpu.SemaphoreType.DMA
    product, stats = pl.pallas_call(
        kernel,
        out_shape=(
            jax.ShapeDtypeStruct((NSUB, OWN, 16, NS), F32),
            jax.ShapeDtypeStruct((8, 128), F32),
        ),
        in_specs=[vmem, smem, vmem, smem, smem, vmem, vmem, vmem, vmem],
        out_specs=(vmem, vmem),
        scratch_shapes=[pltpu.VMEM((GROUPS * MAC, 8, 128), F32) for _ in range(CHUNKS)]
        + [pltpu.VMEM((NSUB, BLK, 8, 128), F32) for _ in range(2 * CHUNKS)]
        + [
            pltpu.VMEM((2, NS, EVENTS * 128), BF16),
            pltpu.VMEM((2, NS, EVENTS * 128), BF16),
            pltpu.VMEM((EVENTS, 2, 384, NS), BF16),
            pltpu.VMEM((EVENTS, NSUB * OWN * 8, NS), F32),
            pltpu.VMEM((OWN, EVENTS * 128, NS), BF16),
            pltpu.VMEM((OWN, EVENTS * 128, NS), BF16),
            pltpu.VMEM((OWN, NS, NS), F32),
            pltpu.VMEM((NSUB, OWN, 16, NS), F32),
            pltpu.VMEM((2, 8, 128), F32),
            pltpu.VMEM((NSUB, 2, 8, 128), F32),
            pltpu.VMEM((GROUPS, 2, 8, 128), F32),
            dma((CHUNKS,)),
            dma((CHUNKS * 16,)),
            dma((CHUNKS,)),
            dma((CHUNKS,)),
            dma((CHUNKS,)),
            dma((CHUNKS,)),
            dma((2,)),
            dma((2,)),
            dma,
            dma,
        ],
        compiler_params=pltpu.CompilerParams(
            collective_id=0, has_side_effects=True, vmem_limit_bytes=56 * 1024 * 1024
        ),
    )(
        macro_state,
        macro_sizes,
        macro_sizes.reshape(8, 128),
        block_sources.T,
        event_rates.T,
        first_factor,
        first_pattern,
        second_factor,
        second_pattern,
    )
    return product.reshape(MAC, 16, NS) * stats[0, 0], stats[1, 0]


def solution(mesh):
    return jax.shard_map(
        on_device,
        mesh=mesh,
        in_specs=(P("grp", "sub", None), P(), P(), P("grp", None), P(), P(), P(), P()),
        out_specs=(P("grp", "sub", None), P()),
        check_vma=False,
    )
```

```python
import jax
import jax.numpy as jnp
from jax import lax
from jax.experimental import pallas as pl
from jax.experimental.pallas import tpu as pltpu
from jax.sharding import PartitionSpec as P

MESH = pl.DeviceIdType.MESH
F32, BF16 = jnp.float32, jnp.bfloat16
NS = 256
EVENTS = 4
NZ = 8
NSUB = 16
MAC = 64
OWN = MAC // NSUB
BLK = OWN * EVENTS
GROUPS = 2 * NZ
PAIRS = MAC // 2
HALF = PAIRS // 2
CHUNKS = 8
STAGGER = 1.0
CW, CCW = 0, 1


def split(x):
    high = x.astype(BF16)
    return high, (x - high.astype(F32)).astype(BF16)


def dot(a, b):
    return jnp.dot(a, b, preferred_element_type=F32)


def kernel(
    state_hbm, sizes_hbm, sizes_vec_ref, sources_hbm, rates_hbm, first_hbm, fpat_hbm, second_hbm, spat_hbm,
    out_ref, stats_ref,
    *scratch,
):
    gathered, outgo, income = scratch[:CHUNKS], scratch[CHUNKS : 2 * CHUNKS], scratch[2 * CHUNKS : 3 * CHUNKS]
    (
        state_ref, sizes_ref, sources_ref, rates_ref, first_ref, fpat_ref, second_ref, spat_ref,
        fh, fl, stc, zacc, zh, zl, pacc, pb, sums, tsub, tgrp,
        load_sem, ring_send, ring_recv, d2d_send, d2d_recv, xy_send, xy_recv, tot_send, tot_recv, out_send, out_recv,
    ) = scratch[3 * CHUNKS :]
    group, piece = lax.axis_index("grp"), lax.axis_index("sub")
    z, core = group // 2, group % 2
    y, x = piece // 4, piece % 4
    sibling = z * 2 + (1 - core)

    def ring_group(distance):
        return ((z + distance + NZ) % NZ) * 2 + core

    def sub_peer(offset):
        return ((y + offset // 4) % 4) * 4 + (x + offset % 4) % 4

    barrier = pltpu.get_barrier_semaphore()

    @pl.loop(1, NSUB)
    def _(offset):
        pl.semaphore_signal(barrier, inc=1, device_id=(group, sub_peer(offset)), device_id_type=MESH)

    @pl.loop(1, GROUPS)
    def _(offset):
        pl.semaphore_signal(barrier, inc=1, device_id=((group + offset) % GROUPS, piece), device_id_type=MESH)

    loads = [
        pltpu.make_async_copy(source, dest, load_sem.at[i])
        for i, (source, dest) in enumerate(
            (
                (state_hbm, state_ref),
                (sizes_hbm, sizes_ref),
                (sources_hbm, sources_ref),
                (rates_hbm, rates_ref),
                (first_hbm, first_ref),
                (fpat_hbm, fpat_ref),
                (second_hbm, second_ref),
                (spat_hbm, spat_ref),
            )
        )
    ]
    for load in loads:
        load.start()

    row_iota = lax.broadcasted_iota(jnp.int32, (8, 128), 0)
    low_lanes = lax.broadcasted_iota(jnp.int32, (8, 128), 1) < 64

    def stage(rh, ch, mass):
        rows = row_iota + (piece * 16 + rh * 8)
        q = rh * 4 + ch * 2

        def masked(m):
            tile = state_ref[m, pl.ds(8 * rh, 8), pl.ds(128 * ch, 128)]
            return jnp.where(rows < sizes_ref[group * MAC + m], tile, 0.0)

        def body(p, mass):
            even, odd = masked(2 * p), masked(2 * p + 1)
            gathered[q][group * PAIRS + p] = jnp.where(low_lanes, even, pltpu.roll(odd, 64, 1))
            gathered[q + 1][group * PAIRS + p] = jnp.where(low_lanes, pltpu.roll(even, 64, 1), odd)
            return mass + even + odd

        return lax.fori_loop(0, PAIRS, body, mass, unroll=8)

    def ring_piece(q, distance, h):
        return gathered[q].at[pl.ds(ring_group(distance) * PAIRS + HALF * h, HALF)]

    def ring_copy(q, way, t, h):
        sign = -1 if way == CW else 1
        part = ring_piece(q, sign * (t - 1), h)
        return pltpu.make_async_remote_copy(
            src_ref=part,
            dst_ref=part,
            send_sem=ring_send.at[q],
            recv_sem=ring_recv.at[((q * 2 + way) * 4 + t - 1) * 2 + h],
            device_id=(ring_group(-sign), piece),
            device_id_type=MESH,
        )

    def ring_wait(q, way, t, h):
        sign = -1 if way == CW else 1
        part = ring_piece(q, sign * t, h)
        pltpu.make_async_copy(part, part, ring_recv.at[((q * 2 + way) * 4 + t - 1) * 2 + h]).wait()

    def sibling_copy(q, part):
        pltpu.make_async_remote_copy(
            src_ref=part,
            dst_ref=part,
            send_sem=d2d_send.at[q],
            recv_sem=d2d_recv.at[q],
            device_id=(sibling, piece),
            device_id_type=MESH,
        ).start()

    def carried(way, t):
        return (0, 1) if t < 4 else ((0,) if way == CW else (1,))

    def ring_start(q):
        for h in (0, 1):
            for way in (CW, CCW):
                ring_copy(q, way, 1, h).start()
        sibling_copy(q, gathered[q].at[pl.ds(group * PAIRS, PAIRS)])

    def ring_step(q, t):
        for h in (0, 1):
            for way in (CW, CCW):
                if h in carried(way, t):
                    ring_wait(q, way, t, h)
                    if t < 4 and h in carried(way, t + 1):
                        ring_copy(q, way, t + 1, h).start()
                    sibling_copy(q, ring_piece(q, -t if way == CW else t, h))

    def prepare(k):
        rows_of = (lax.broadcasted_iota(jnp.int32, (NS, 16), 0) // 16 == lax.broadcasted_iota(jnp.int32, (NS, 16), 1))
        cols_of = (lax.broadcasted_iota(jnp.int32, (16, NS), 1) // 16 == lax.broadcasted_iota(jnp.int32, (16, NS), 0))
        rows_of, cols_of = rows_of.astype(F32).astype(BF16), cols_of.astype(F32).astype(BF16)

        def widen(pattern):
            return dot(dot(rows_of, pattern.astype(F32).astype(BF16)).astype(BF16), cols_of)

        source = lax.broadcasted_iota(jnp.int32, (NS, NS), 0)
        target = lax.broadcasted_iota(jnp.int32, (NS, NS), 1)
        place = (source // 8 % 2) * 128 + (source // 16) * 8 + source % 8
        order = (place == target).astype(F32).astype(BF16)
        high, low = split(first_ref[k] * widen(fpat_ref[k]))
        for part, dest in ((high, fh), (low, fl)):
            moved = dot(part, order).astype(BF16)
            for rh in (0, 1):
                dest[rh, :, k * 128 : (k + 1) * 128] = moved[:, rh * 128 : (rh + 1) * 128]
        high, low = split((second_ref[k] * widen(spat_ref[k])).T)
        zeros = jnp.zeros((64, NS), BF16)
        for cq in range(4):
            rows = slice(cq * 64, cq * 64 + 64)
            for third, part in enumerate((high[rows], low[rows], high[rows])):
                at = third * 128
                stc[k, cq, at : at + 64, :NS] = part
                stc[k, cq, at : at + 64, NS:] = zeros
                stc[k, cq, at + 64 : at + 128, :NS] = zeros
                stc[k, cq, at + 64 : at + 128, NS:] = part

    def select(q):
        part = gathered[q].at[pl.ds(0, GROUPS // 2 * PAIRS)]
        pltpu.make_async_copy(part, part, d2d_recv.at[q]).wait()

        def pick(j, dest, at):
            tiles = []
            for k in range(EVENTS):
                for u in range(OWN // 2):
                    even = sources_ref[k, group * MAC + j * OWN + 2 * u]
                    odd = sources_ref[k, group * MAC + j * OWN + 2 * u + 1]
                    one, two = gathered[q][even // 2], gathered[q][odd // 2]
                    one = jnp.where(even % 2 == 0, one, pltpu.roll(one, 64, 1))
                    two = jnp.where(odd % 2 == 0, pltpu.roll(two, 64, 1), two)
                    tiles.append(jnp.where(low_lanes, one, two))
            for b, tile in enumerate(tiles):
                dest[at, b] = tile

        @pl.loop(1, NSUB)
        def _(offset):
            j = sub_peer(offset)
            pick(j, outgo[q], j)
            pltpu.make_async_remote_copy(
                src_ref=outgo[q].at[j],
                dst_ref=income[q].at[piece],
                send_sem=xy_send.at[q],
                recv_sem=xy_recv.at[q],
                device_id=(group, j),
                device_id_type=MESH,
            ).start()

        pick(piece, income[q], piece)

    def stage1(q):
        rh, cq = q // 4, q % 4
        part = income[q].at[pl.ds(0, NSUB - 1)]
        pltpu.make_async_copy(part, part, xy_recv.at[q]).wait()
        for k in range(EVENTS):
            block = income[q][:, k * OWN // 2 : (k + 1) * OWN // 2].reshape(NSUB * OWN // 2 * 8, 128)
            high, low = split(block)
            part = dot(jnp.concatenate([high, high, low], axis=1), stc[k, cq])
            if cq > 0:
                part = part + zacc[k]
            if cq < 3:
                zacc[k] = part
            else:
                for mm in range(OWN):
                    rate = rates_ref[k, piece * OWN + mm]
                    half = part[:, mm % 2 * NS : mm % 2 * NS + NS].reshape(NSUB, OWN // 2, 8, NS)
                    high, low = split(half[:, mm // 2].reshape(128, NS) * rate)
                    zh[mm, k * 128 : (k + 1) * 128, :] = high
                    zl[mm, k * 128 : (k + 1) * 128, :] = low

    def stage2(mm, rh):
        high, low = zh[mm], zl[mm]
        return dot(fh[rh], high) + dot(fh[rh], low) + dot(fl[rh], high)

    loads[0].wait()
    loads[1].wait()
    mass = stage(0, 0, jnp.zeros((8, 128), F32))
    pl.semaphore_wait(barrier, NSUB - 1 + GROUPS - 1)
    ring_start(0)
    mass = stage(0, 1, mass)

    events = sorted((q * STAGGER + t, q, t) for q in range(CHUNKS) for t in range(1, 5))
    started, due, todo = 1, [], list(range(EVENTS))
    for now, q, t in events:
        while started < CHUNKS and started * STAGGER <= now - 1:
            ring_start(started)
            started += 1
        ring_step(q, t)
        if (q, t) == (0, 1):
            mass = stage(1, 0, mass)
            mass = stage(1, 1, mass)
            sums[1] = mass
            for load in loads[2:]:
                load.wait()
        elif todo:
            prepare(todo.pop(0))
        for task in due:
            select(task)
            if task > 0:
                stage1(task - 1)
            if task == 4:
                for mm in range(OWN):
                    pacc[mm] = stage2(mm, 0)
        due = [q] if t == 4 else []

    select(CHUNKS - 1)
    stage1(CHUNKS - 2)
    stage1(CHUNKS - 1)

    all_rows = lax.broadcasted_iota(jnp.int32, (NS, NS), 0)
    total = jnp.zeros((8, NS), F32)
    for mm in range(OWN):
        size = sizes_ref[group * MAC + piece * OWN + mm]
        product = jnp.where(all_rows < size, pacc[mm] + stage2(mm, 1), 0.0)
        total = total + jnp.sum(product.reshape(NS // 8, 8, NS), axis=0)
        pb[:, mm] = product.reshape(NSUB, 16, NS)
    sums[0] = total[:, :128] + total[:, 128:]

    tsub[piece] = sums[...]

    @pl.loop(1, NSUB)
    def _(offset):
        pltpu.make_async_remote_copy(
            src_ref=sums,
            dst_ref=tsub.at[piece],
            send_sem=tot_send.at[0],
            recv_sem=tot_recv.at[0],
            device_id=(group, sub_peer(offset)),
            device_id_type=MESH,
        ).start()

    @pl.loop(1, NSUB)
    def _(offset):
        j = sub_peer(offset)
        pltpu.make_async_remote_copy(
            src_ref=pb.at[j],
            dst_ref=out_ref.at[piece],
            send_sem=out_send,
            recv_sem=out_recv,
            device_id=(group, j),
            device_id_type=MESH,
        ).start()

    out_ref[piece] = pb[piece]
    pltpu.make_async_copy(tsub.at[pl.ds(0, NSUB - 1)], tsub.at[pl.ds(0, NSUB - 1)], tot_recv.at[0]).wait()
    tgrp[group] = jnp.sum(tsub[...], axis=0)

    @pl.loop(1, GROUPS)
    def _(offset):
        pltpu.make_async_remote_copy(
            src_ref=tgrp.at[group],
            dst_ref=tgrp.at[group],
            send_sem=tot_send.at[1],
            recv_sem=tot_recv.at[1],
            device_id=((group + offset) % GROUPS, piece),
            device_id_type=MESH,
        ).start()

    for q in range(CHUNKS):
        part = gathered[q].at[pl.ds(0, 14 * HALF)]
        pltpu.make_async_copy(part, part, ring_send.at[q]).wait()
        part = gathered[q].at[pl.ds(0, PAIRS + 14 * HALF)]
        pltpu.make_async_copy(part, part, d2d_send.at[q]).wait()
        part = outgo[q].at[pl.ds(0, NSUB - 1)]
        pltpu.make_async_copy(part, part, xy_send.at[q]).wait()
    part = tsub.at[pl.ds(0, NSUB - 1)]
    pltpu.make_async_copy(part, part, tot_send.at[0]).wait()
    live = jnp.sum(sizes_vec_ref[...].astype(F32)) * NS

    part = tgrp.at[pl.ds(0, GROUPS - 1)]
    pltpu.make_async_copy(part, part, tot_recv.at[1]).wait()
    both = jnp.sum(tgrp[...], axis=0)
    total, mass = jnp.sum(both[0]), jnp.sum(both[1])
    pick = lax.broadcasted_iota(jnp.int32, (8, 128), 0) == 0
    numer = jnp.where(pick, jnp.full((8, 128), live, F32), jnp.full((8, 128), total, F32))
    denom = jnp.where(pick, jnp.full((8, 128), total, F32), jnp.full((8, 128), mass, F32))
    stats_ref[...] = numer / denom

    pltpu.make_async_copy(part, part, tot_send.at[1]).wait()
    part = pb.at[pl.ds(0, NSUB - 1)]
    pltpu.make_async_copy(part, part, out_recv).wait()
    pltpu.make_async_copy(part, part, out_send).wait()


def rescale(product_ref, stats_ref, scaled_ref, growth_ref):
    scaled_ref[...] = product_ref[...] * stats_ref[0:1, 0:1].reshape(1, 1, 1)
    growth_ref[...] = stats_ref[1:2, 0:1]


def on_device(
    macro_state, macro_sizes, block_sources, event_rates, first_factor, first_pattern, second_factor, second_pattern
):
    vmem, hbm = pl.BlockSpec(memory_space=pltpu.VMEM), pl.BlockSpec(memory_space=pltpu.HBM)
    dma = pltpu.SemaphoreType.DMA
    product, stats = pl.pallas_call(
        kernel,
        out_shape=(
            pltpu.VMEM((NSUB, OWN, 16, NS), F32),
            pltpu.VMEM((8, 128), F32),
        ),
        in_specs=[hbm, hbm, vmem, hbm, hbm, hbm, hbm, hbm, hbm],
        out_specs=(vmem, vmem),
        scratch_shapes=[pltpu.VMEM((GROUPS * PAIRS, 8, 128), F32) for _ in range(CHUNKS)]
        + [pltpu.VMEM((NSUB, BLK // 2, 8, 128), F32) for _ in range(2 * CHUNKS)]
        + [
            pltpu.VMEM((MAC, 16, NS), F32),
            pltpu.SMEM((GROUPS * MAC,), jnp.int32),
            pltpu.SMEM((EVENTS, GROUPS * MAC), jnp.int32),
            pltpu.SMEM((EVENTS, MAC), F32),
            pltpu.VMEM((EVENTS, NS, NS), F32),
            pltpu.VMEM((EVENTS, 16, 16), jnp.int32),
            pltpu.VMEM((EVENTS, NS, NS), F32),
            pltpu.VMEM((EVENTS, 16, 16), jnp.int32),
            pltpu.VMEM((2, NS, EVENTS * 128), BF16),
            pltpu.VMEM((2, NS, EVENTS * 128), BF16),
            pltpu.VMEM((EVENTS, 4, 384, 2 * NS), BF16),
            pltpu.VMEM((EVENTS, NSUB * OWN // 2 * 8, 2 * NS), F32),
            pltpu.VMEM((OWN, EVENTS * 128, NS), BF16),
            pltpu.VMEM((OWN, EVENTS * 128, NS), BF16),
            pltpu.VMEM((OWN, NS, NS), F32),
            pltpu.VMEM((NSUB, OWN, 16, NS), F32),
            pltpu.VMEM((2, 8, 128), F32),
            pltpu.VMEM((NSUB, 2, 8, 128), F32),
            pltpu.VMEM((GROUPS, 2, 8, 128), F32),
            dma((8,)),
            dma((CHUNKS,)),
            dma((CHUNKS * 16,)),
            dma((CHUNKS,)),
            dma((CHUNKS,)),
            dma((CHUNKS,)),
            dma((CHUNKS,)),
            dma((2,)),
            dma((2,)),
            dma,
            dma,
        ],
        compiler_params=pltpu.CompilerParams(
            collective_id=0, has_side_effects=True, vmem_limit_bytes=56 * 1024 * 1024
        ),
    )(
        macro_state,
        macro_sizes,
        macro_sizes.reshape(8, 128),
        block_sources.T,
        event_rates.T,
        first_factor,
        first_pattern,
        second_factor,
        second_pattern,
    )
    scaled, growth = pl.pallas_call(
        rescale,
        out_shape=(
            jax.ShapeDtypeStruct((MAC, 16, NS), F32),
            jax.ShapeDtypeStruct((1, 1), F32),
        ),
        in_specs=[vmem, vmem],
        out_specs=(vmem, vmem),
    )(
        pltpu.with_memory_space_constraint(product.reshape(MAC, 16, NS), pltpu.VMEM),
        pltpu.with_memory_space_constraint(stats, pltpu.VMEM),
    )
    return scaled, growth.reshape(())


def solution(mesh):
    return jax.shard_map(
        on_device,
        mesh=mesh,
        in_specs=(P("grp", "sub", None), P(), P(), P("grp", None), P(), P(), P(), P()),
        out_specs=(P("grp", "sub", None), P()),
        check_vma=False,
    )
```

```python
import functools

import jax
import jax.numpy as jnp
from jax import lax
from jax.experimental import pallas as pl
from jax.experimental.pallas import tpu as pltpu
from jax.sharding import PartitionSpec as P

MESH = pl.DeviceIdType.MESH
F32, BF16 = jnp.float32, jnp.bfloat16
NS = 256
EVENTS = 4
NZ = 8
NSUB = 16
MAC = 64
OWN = MAC // NSUB
BLK = OWN * EVENTS
GROUPS = 2 * NZ
PAIRS = MAC // 2
HALF = PAIRS // 2
CHUNKS = 8
DELAY = 2
LAG = 6
BURST = 1
STAGGER = 1.0
CW, CCW = 0, 1


def split(x):
    high = x.astype(BF16)
    return high, (x - high.astype(F32)).astype(BF16)


def dot(a, b):
    return jnp.dot(a, b, preferred_element_type=F32)


def kernel(
    state_hbm, sizes_hbm, sizes_vec_ref, sources_hbm, rates_hbm, first_hbm, fpat_hbm, second_hbm, spat_hbm,
    out_ref, stats_ref,
    *scratch,
):
    gathered, outgo, income = scratch[:CHUNKS], scratch[CHUNKS : 2 * CHUNKS], scratch[2 * CHUNKS : 3 * CHUNKS]
    (
        state_ref, sizes_ref, sources_ref, rates_ref, first_ref, fpat_ref, second_ref, spat_ref,
        fh, fl, stc, zacc, zh, zl, pacc, pb, sums, tsub, tgrp,
        load_sem, ring_send, ring_recv, d2d_send, d2d_recv, xy_send, xy_recv, tot_send, tot_recv, out_send, out_recv,
    ) = scratch[3 * CHUNKS :]
    group, piece = lax.axis_index("grp"), lax.axis_index("sub")
    z, core = group // 2, group % 2
    y, x = piece // 4, piece % 4
    sibling = z * 2 + (1 - core)

    def ring_group(distance):
        return ((z + distance + NZ) % NZ) * 2 + core

    def sub_peer(offset):
        return ((y + offset // 4) % 4) * 4 + (x + offset % 4) % 4

    barrier = pltpu.get_barrier_semaphore()

    @pl.loop(1, NSUB)
    def _(offset):
        pl.semaphore_signal(barrier, inc=1, device_id=(group, sub_peer(offset)), device_id_type=MESH)

    @pl.loop(1, GROUPS)
    def _(offset):
        pl.semaphore_signal(barrier, inc=1, device_id=((group + offset) % GROUPS, piece), device_id_type=MESH)

    loads = [
        pltpu.make_async_copy(source, dest, load_sem.at[i])
        for i, (source, dest) in enumerate(
            (
                (state_hbm, state_ref),
                (sizes_hbm, sizes_ref),
                (sources_hbm, sources_ref),
                (rates_hbm, rates_ref),
                (first_hbm, first_ref),
                (fpat_hbm, fpat_ref),
                (second_hbm, second_ref),
                (spat_hbm, spat_ref),
            )
        )
    ]
    for load in loads:
        load.start()

    row_iota = lax.broadcasted_iota(jnp.int32, (8, 128), 0)
    low_lanes = lax.broadcasted_iota(jnp.int32, (8, 128), 1) < 64

    def stage(rh, ch, mass):
        rows = row_iota + (piece * 16 + rh * 8)
        q = rh * 4 + ch * 2

        def masked(m):
            tile = state_ref[m, pl.ds(8 * rh, 8), pl.ds(128 * ch, 128)]
            return jnp.where(rows < sizes_ref[group * MAC + m], tile, 0.0)

        def body(p, mass):
            even, odd = masked(2 * p), masked(2 * p + 1)
            gathered[q][group * PAIRS + p] = jnp.where(low_lanes, even, pltpu.roll(odd, 64, 1))
            gathered[q + 1][group * PAIRS + p] = jnp.where(low_lanes, pltpu.roll(even, 64, 1), odd)
            return mass + even + odd

        return lax.fori_loop(0, PAIRS, body, mass, unroll=8)

    def ring_piece(q, distance, h):
        return gathered[q].at[pl.ds(ring_group(distance) * PAIRS + HALF * h, HALF)]

    def ring_copy(q, way, t, h):
        sign = -1 if way == CW else 1
        part = ring_piece(q, sign * (t - 1), h)
        return pltpu.make_async_remote_copy(
            src_ref=part,
            dst_ref=part,
            send_sem=ring_send.at[q],
            recv_sem=ring_recv.at[((q * 2 + way) * 4 + t - 1) * 2 + h],
            device_id=(ring_group(-sign), piece),
            device_id_type=MESH,
        )

    def ring_wait(q, way, t, h):
        sign = -1 if way == CW else 1
        part = ring_piece(q, sign * t, h)
        pltpu.make_async_copy(part, part, ring_recv.at[((q * 2 + way) * 4 + t - 1) * 2 + h]).wait()

    def sibling_copy(q, part):
        pltpu.make_async_remote_copy(
            src_ref=part,
            dst_ref=part,
            send_sem=d2d_send.at[q],
            recv_sem=d2d_recv.at[q],
            device_id=(sibling, piece),
            device_id_type=MESH,
        ).start()

    def carried(way, t):
        return (0, 1) if t < 4 else ((0,) if way == CW else (1,))

    def ring_start(q):
        for h in (0, 1):
            for way in (CW, CCW):
                ring_copy(q, way, 1, h).start()
        sibling_copy(q, gathered[q].at[pl.ds(group * PAIRS, PAIRS)])

    def ring_step(q, t):
        for h in (0, 1):
            for way in (CW, CCW):
                if h in carried(way, t):
                    ring_wait(q, way, t, h)
                    if t < 4 and h in carried(way, t + 1):
                        ring_copy(q, way, t + 1, h).start()
                    sibling_copy(q, ring_piece(q, -t if way == CW else t, h))

    def prepare(k):
        rows_of = (lax.broadcasted_iota(jnp.int32, (NS, 16), 0) // 16 == lax.broadcasted_iota(jnp.int32, (NS, 16), 1))
        cols_of = (lax.broadcasted_iota(jnp.int32, (16, NS), 1) // 16 == lax.broadcasted_iota(jnp.int32, (16, NS), 0))
        rows_of, cols_of = rows_of.astype(F32).astype(BF16), cols_of.astype(F32).astype(BF16)

        def widen(pattern):
            return dot(dot(rows_of, pattern.astype(F32).astype(BF16)).astype(BF16), cols_of)

        source = lax.broadcasted_iota(jnp.int32, (NS, NS), 0)
        target = lax.broadcasted_iota(jnp.int32, (NS, NS), 1)
        place = (source // 8 % 2) * 128 + (source // 16) * 8 + source % 8
        order = (place == target).astype(F32).astype(BF16)
        high, low = split(first_ref[k] * widen(fpat_ref[k]))
        for part, dest in ((high, fh), (low, fl)):
            moved = dot(part, order).astype(BF16)
            for rh in (0, 1):
                dest[rh, :, k * 128 : (k + 1) * 128] = moved[:, rh * 128 : (rh + 1) * 128]
        high, low = split((second_ref[k] * widen(spat_ref[k])).T)
        zeros = jnp.zeros((64, NS), BF16)
        for cq in range(4):
            rows = slice(cq * 64, cq * 64 + 64)
            for third, part in enumerate((high[rows], low[rows], high[rows])):
                at = third * 128
                stc[k, cq, at : at + 64, :NS] = part
                stc[k, cq, at : at + 64, NS:] = zeros
                stc[k, cq, at + 64 : at + 128, :NS] = zeros
                stc[k, cq, at + 64 : at + 128, NS:] = part

    def select(q, first, last):
        if first == 1:
            part = gathered[q].at[pl.ds(0, GROUPS // 2 * PAIRS)]
            pltpu.make_async_copy(part, part, d2d_recv.at[q]).wait()

        def pick(j, dest, at):
            tiles = []
            for k in range(EVENTS):
                for u in range(OWN // 2):
                    even = sources_ref[k, group * MAC + j * OWN + 2 * u]
                    odd = sources_ref[k, group * MAC + j * OWN + 2 * u + 1]
                    one = pltpu.roll(gathered[q][lax.shift_right_logical(even, 1)], (even & 1) * 64, 1)
                    two = pltpu.roll(gathered[q][lax.shift_right_logical(odd, 1)], 64 - (odd & 1) * 64, 1)
                    tiles.append(jnp.where(low_lanes, one, two))
            for b, tile in enumerate(tiles):
                dest[at, b] = tile

        @pl.loop(first, last)
        def _(offset):
            j = sub_peer(offset)
            pick(j, outgo[q], j)
            pltpu.make_async_remote_copy(
                src_ref=outgo[q].at[j],
                dst_ref=income[q].at[piece],
                send_sem=xy_send.at[q],
                recv_sem=xy_recv.at[q],
                device_id=(group, j),
                device_id_type=MESH,
            ).start()

        if last == NSUB:
            pick(piece, income[q], piece)

    def stage1(q, events):
        rh, cq = q // 4, q % 4
        if events[0] == 0:
            part = income[q].at[pl.ds(0, NSUB - 1)]
            pltpu.make_async_copy(part, part, xy_recv.at[q]).wait()
        for k in events:
            block = income[q][:, k * OWN // 2 : (k + 1) * OWN // 2].reshape(NSUB * OWN // 2 * 8, 128)
            high, low = split(block)
            part = dot(jnp.concatenate([high, high, low], axis=1), stc[k, cq])
            if cq > 0:
                part = part + zacc[k]
            if cq < 3:
                zacc[k] = part
            else:
                for mm in range(OWN):
                    rate = rates_ref[k, piece * OWN + mm]
                    half = part[:, mm % 2 * NS : mm % 2 * NS + NS].reshape(NSUB, OWN // 2, 8, NS)
                    high, low = split(half[:, mm // 2].reshape(128, NS) * rate)
                    zh[mm, k * 128 : (k + 1) * 128, :] = high
                    zl[mm, k * 128 : (k + 1) * 128, :] = low

    def stage2(mm, rh):
        high, low = zh[mm], zl[mm]
        return dot(fh[rh], high) + dot(fh[rh], low) + dot(fl[rh], high)

    loads[0].wait()
    loads[1].wait()
    mass = stage(0, 0, jnp.zeros((8, 128), F32))
    pl.semaphore_wait(barrier, NSUB - 1 + GROUPS - 1)
    ring_start(0)
    mass = stage(0, 1, mass)

    def finish_stage(mass):
        mass = stage(1, 1, stage(1, 0, mass))
        sums[1] = mass
        for load in loads[2:]:
            load.wait()

    def first_product(mm):
        pacc[mm] = stage2(mm, 0)

    picks, products = [], [(0, functools.partial(prepare, k)) for k in range(EVENTS)]
    started = 1
    steps = sorted((q * STAGGER + t, q, t) for q in range(CHUNKS) for t in range(1, 5))
    for at, (now, q, t) in enumerate(steps):
        while started < CHUNKS and started * STAGGER <= now - 1:
            ring_start(started)
            started += 1
        ring_step(q, t)
        if at == 0:
            finish_stage(mass)
            continue
        for _ in range(BURST):
            for queue in (picks, products):
                if queue and queue[0][0] <= at:
                    queue.pop(0)[1]()
                    break
        if t == 4:
            picks.append((at + DELAY, functools.partial(select, q, 1, NSUB // 2)))
            picks.append((at + DELAY, functools.partial(select, q, NSUB // 2, NSUB)))
            products.append((at + DELAY + LAG, functools.partial(stage1, q, (0, 1))))
            products.append((at + DELAY + LAG, functools.partial(stage1, q, (2, 3))))
            if q == 3:
                products.extend((0, functools.partial(first_product, mm)) for mm in range(OWN))

    for _, task in picks + products:
        task()

    all_rows = lax.broadcasted_iota(jnp.int32, (NS, NS), 0)
    total = jnp.zeros((8, NS), F32)
    for mm in range(OWN):
        size = sizes_ref[group * MAC + piece * OWN + mm]
        product = jnp.where(all_rows < size, pacc[mm] + stage2(mm, 1), 0.0)
        total = total + jnp.sum(product.reshape(NS // 8, 8, NS), axis=0)
        pb[:, mm] = product.reshape(NSUB, 16, NS)
    sums[0] = total[:, :128] + total[:, 128:]

    tsub[piece] = sums[...]

    @pl.loop(1, NSUB)
    def _(offset):
        pltpu.make_async_remote_copy(
            src_ref=sums,
            dst_ref=tsub.at[piece],
            send_sem=tot_send.at[0],
            recv_sem=tot_recv.at[0],
            device_id=(group, sub_peer(offset)),
            device_id_type=MESH,
        ).start()

    @pl.loop(1, NSUB)
    def _(offset):
        j = sub_peer(offset)
        pltpu.make_async_remote_copy(
            src_ref=pb.at[j],
            dst_ref=out_ref.at[piece],
            send_sem=out_send,
            recv_sem=out_recv,
            device_id=(group, j),
            device_id_type=MESH,
        ).start()

    out_ref[piece] = pb[piece]
    pltpu.make_async_copy(tsub.at[pl.ds(0, NSUB - 1)], tsub.at[pl.ds(0, NSUB - 1)], tot_recv.at[0]).wait()
    tgrp[group] = jnp.sum(tsub[...], axis=0)

    @pl.loop(1, GROUPS)
    def _(offset):
        pltpu.make_async_remote_copy(
            src_ref=tgrp.at[group],
            dst_ref=tgrp.at[group],
            send_sem=tot_send.at[1],
            recv_sem=tot_recv.at[1],
            device_id=((group + offset) % GROUPS, piece),
            device_id_type=MESH,
        ).start()

    for q in range(CHUNKS):
        part = gathered[q].at[pl.ds(0, 14 * HALF)]
        pltpu.make_async_copy(part, part, ring_send.at[q]).wait()
        part = gathered[q].at[pl.ds(0, PAIRS + 14 * HALF)]
        pltpu.make_async_copy(part, part, d2d_send.at[q]).wait()
        part = outgo[q].at[pl.ds(0, NSUB - 1)]
        pltpu.make_async_copy(part, part, xy_send.at[q]).wait()
    part = tsub.at[pl.ds(0, NSUB - 1)]
    pltpu.make_async_copy(part, part, tot_send.at[0]).wait()
    live = jnp.sum(sizes_vec_ref[...].astype(F32)) * NS

    part = tgrp.at[pl.ds(0, GROUPS - 1)]
    pltpu.make_async_copy(part, part, tot_recv.at[1]).wait()
    both = jnp.sum(tgrp[...], axis=0)
    total, mass = jnp.sum(both[0]), jnp.sum(both[1])
    pick = lax.broadcasted_iota(jnp.int32, (8, 128), 0) == 0
    numer = jnp.where(pick, jnp.full((8, 128), live, F32), jnp.full((8, 128), total, F32))
    denom = jnp.where(pick, jnp.full((8, 128), total, F32), jnp.full((8, 128), mass, F32))
    stats_ref[...] = numer / denom

    pltpu.make_async_copy(part, part, tot_send.at[1]).wait()
    part = pb.at[pl.ds(0, NSUB - 1)]
    pltpu.make_async_copy(part, part, out_recv).wait()
    pltpu.make_async_copy(part, part, out_send).wait()


def rescale(product_ref, stats_ref, scaled_ref, growth_ref):
    scaled_ref[...] = product_ref[...] * stats_ref[0:1, 0:1].reshape(1, 1, 1)
    growth_ref[...] = stats_ref[1:2, 0:1]


def on_device(
    macro_state, macro_sizes, block_sources, event_rates, first_factor, first_pattern, second_factor, second_pattern
):
    vmem, hbm = pl.BlockSpec(memory_space=pltpu.VMEM), pl.BlockSpec(memory_space=pltpu.HBM)
    dma = pltpu.SemaphoreType.DMA
    product, stats = pl.pallas_call(
        kernel,
        out_shape=(
            pltpu.VMEM((NSUB, OWN, 16, NS), F32),
            pltpu.VMEM((8, 128), F32),
        ),
        in_specs=[hbm, hbm, vmem, hbm, hbm, hbm, hbm, hbm, hbm],
        out_specs=(vmem, vmem),
        scratch_shapes=[pltpu.VMEM((GROUPS * PAIRS, 8, 128), F32) for _ in range(CHUNKS)]
        + [pltpu.VMEM((NSUB, BLK // 2, 8, 128), F32) for _ in range(2 * CHUNKS)]
        + [
            pltpu.VMEM((MAC, 16, NS), F32),
            pltpu.SMEM((GROUPS * MAC,), jnp.int32),
            pltpu.SMEM((EVENTS, GROUPS * MAC), jnp.int32),
            pltpu.SMEM((EVENTS, MAC), F32),
            pltpu.VMEM((EVENTS, NS, NS), F32),
            pltpu.VMEM((EVENTS, 16, 16), jnp.int32),
            pltpu.VMEM((EVENTS, NS, NS), F32),
            pltpu.VMEM((EVENTS, 16, 16), jnp.int32),
            pltpu.VMEM((2, NS, EVENTS * 128), BF16),
            pltpu.VMEM((2, NS, EVENTS * 128), BF16),
            pltpu.VMEM((EVENTS, 4, 384, 2 * NS), BF16),
            pltpu.VMEM((EVENTS, NSUB * OWN // 2 * 8, 2 * NS), F32),
            pltpu.VMEM((OWN, EVENTS * 128, NS), BF16),
            pltpu.VMEM((OWN, EVENTS * 128, NS), BF16),
            pltpu.VMEM((OWN, NS, NS), F32),
            pltpu.VMEM((NSUB, OWN, 16, NS), F32),
            pltpu.VMEM((2, 8, 128), F32),
            pltpu.VMEM((NSUB, 2, 8, 128), F32),
            pltpu.VMEM((GROUPS, 2, 8, 128), F32),
            dma((8,)),
            dma((CHUNKS,)),
            dma((CHUNKS * 16,)),
            dma((CHUNKS,)),
            dma((CHUNKS,)),
            dma((CHUNKS,)),
            dma((CHUNKS,)),
            dma((2,)),
            dma((2,)),
            dma,
            dma,
        ],
        compiler_params=pltpu.CompilerParams(
            collective_id=0, has_side_effects=True, vmem_limit_bytes=56 * 1024 * 1024
        ),
    )(
        macro_state,
        macro_sizes,
        macro_sizes.reshape(8, 128),
        block_sources.T,
        event_rates.T,
        first_factor,
        first_pattern,
        second_factor,
        second_pattern,
    )
    scaled, growth = pl.pallas_call(
        rescale,
        out_shape=(
            jax.ShapeDtypeStruct((MAC, 16, NS), F32),
            jax.ShapeDtypeStruct((1, 1), F32),
        ),
        in_specs=[vmem, vmem],
        out_specs=(vmem, vmem),
    )(
        pltpu.with_memory_space_constraint(product.reshape(MAC, 16, NS), pltpu.VMEM),
        pltpu.with_memory_space_constraint(stats, pltpu.VMEM),
    )
    return scaled, growth.reshape(())


def solution(mesh):
    return jax.shard_map(
        on_device,
        mesh=mesh,
        in_specs=(P("grp", "sub", None), P(), P(), P("grp", None), P(), P(), P(), P()),
        out_specs=(P("grp", "sub", None), P()),
        check_vma=False,
    )
```

```python
import functools

import jax
import jax.numpy as jnp
from jax import lax
from jax.experimental import pallas as pl
from jax.experimental.pallas import tpu as pltpu
from jax.sharding import PartitionSpec as P

MESH = pl.DeviceIdType.MESH
F32, BF16 = jnp.float32, jnp.bfloat16
NS = 256
EVENTS = 4
NZ = 8
NSUB = 16
MAC = 64
OWN = MAC // NSUB
BLK = OWN * EVENTS
GROUPS = 2 * NZ
PAIRS = MAC // 2
HALF = PAIRS // 2
CHUNKS = 8
DELAY = 2
LAG = 6
BURST = 1
STAGGER = 1.0
CW, CCW = 0, 1


def split(x):
    high = x.astype(BF16)
    return high, (x - high.astype(F32)).astype(BF16)


def dot(a, b):
    return jnp.dot(a, b, preferred_element_type=F32)


def kernel(
    state_hbm, sizes_hbm, sizes_vec_ref, sources_hbm, rates_hbm, first_hbm, fpat_hbm, second_hbm, spat_hbm,
    out_ref, stats_ref,
    *scratch,
):
    gathered, outgo, income = scratch[:CHUNKS], scratch[CHUNKS : 2 * CHUNKS], scratch[2 * CHUNKS : 3 * CHUNKS]
    (
        state_ref, sizes_ref, sources_ref, rates_ref, first_ref, fpat_ref, second_ref, spat_ref,
        fh, fl, stc, zacc, zh, zl, pacc, pb, sums, tsub, tgrp,
        load_sem, ring_send, ring_recv, d2d_send, d2d_recv, xy_send, xy_recv, tot_send, tot_recv, out_send, out_recv,
    ) = scratch[3 * CHUNKS :]
    group, piece = lax.axis_index("grp"), lax.axis_index("sub")
    z, core = group // 2, group % 2
    y, x = piece // 4, piece % 4
    sibling = z * 2 + (1 - core)

    def ring_group(distance):
        return ((z + distance + NZ) % NZ) * 2 + core

    def sub_peer(offset):
        return ((y + offset // 4) % 4) * 4 + (x + offset % 4) % 4

    barrier = pltpu.get_barrier_semaphore()

    @pl.loop(1, NSUB)
    def _(offset):
        pl.semaphore_signal(barrier, inc=1, device_id=(group, sub_peer(offset)), device_id_type=MESH)

    @pl.loop(1, GROUPS)
    def _(offset):
        pl.semaphore_signal(barrier, inc=1, device_id=((group + offset) % GROUPS, piece), device_id_type=MESH)

    loads = [
        pltpu.make_async_copy(source, dest, load_sem.at[i])
        for i, (source, dest) in enumerate(
            (
                (state_hbm, state_ref),
                (sizes_hbm, sizes_ref),
                (sources_hbm, sources_ref),
                (rates_hbm, rates_ref),
                (first_hbm, first_ref),
                (fpat_hbm, fpat_ref),
                (second_hbm, second_ref),
                (spat_hbm, spat_ref),
            )
        )
    ]
    for load in loads:
        load.start()

    row_iota = lax.broadcasted_iota(jnp.int32, (8, 128), 0)
    low_lanes = lax.broadcasted_iota(jnp.int32, (8, 128), 1) < 64

    def stage(rh, ch, mass):
        rows = row_iota + (piece * 16 + rh * 8)
        q = rh * 4 + ch * 2

        def masked(m):
            tile = state_ref[m, pl.ds(8 * rh, 8), pl.ds(128 * ch, 128)]
            return jnp.where(rows < sizes_ref[group * MAC + m], tile, 0.0)

        def body(p, mass):
            even, odd = masked(2 * p), masked(2 * p + 1)
            gathered[q][group * PAIRS + p] = jnp.where(low_lanes, even, pltpu.roll(odd, 64, 1))
            gathered[q + 1][group * PAIRS + p] = jnp.where(low_lanes, pltpu.roll(even, 64, 1), odd)
            return mass + even + odd

        return lax.fori_loop(0, PAIRS, body, mass, unroll=8)

    def ring_piece(q, distance, h):
        return gathered[q].at[pl.ds(ring_group(distance) * PAIRS + HALF * h, HALF)]

    def ring_copy(q, way, t, h):
        sign = -1 if way == CW else 1
        part = ring_piece(q, sign * (t - 1), h)
        return pltpu.make_async_remote_copy(
            src_ref=part,
            dst_ref=part,
            send_sem=ring_send.at[q],
            recv_sem=ring_recv.at[((q * 2 + way) * 4 + t - 1) * 2 + h],
            device_id=(ring_group(-sign), piece),
            device_id_type=MESH,
        )

    def ring_wait(q, way, t, h):
        sign = -1 if way == CW else 1
        part = ring_piece(q, sign * t, h)
        pltpu.make_async_copy(part, part, ring_recv.at[((q * 2 + way) * 4 + t - 1) * 2 + h]).wait()

    def sibling_copy(q, part):
        pltpu.make_async_remote_copy(
            src_ref=part,
            dst_ref=part,
            send_sem=d2d_send.at[q],
            recv_sem=d2d_recv.at[q],
            device_id=(sibling, piece),
            device_id_type=MESH,
        ).start()

    def carried(way, t):
        return (0, 1) if t < 4 else ((0,) if way == CW else (1,))

    def ring_start(q):
        for h in (0, 1):
            for way in (CW, CCW):
                ring_copy(q, way, 1, h).start()
        sibling_copy(q, gathered[q].at[pl.ds(group * PAIRS, PAIRS)])

    def ring_step(q, t):
        for h in (0, 1):
            for way in (CW, CCW):
                if h in carried(way, t):
                    ring_wait(q, way, t, h)
                    if t < 4 and h in carried(way, t + 1):
                        ring_copy(q, way, t + 1, h).start()
                    if t == 4:
                        sibling_copy(q, ring_piece(q, -t if way == CW else t, h))
                    elif h == 1:
                        sibling_copy(q, gathered[q].at[pl.ds(ring_group(-t if way == CW else t) * PAIRS, PAIRS)])

    def prepare(k):
        rows_of = (lax.broadcasted_iota(jnp.int32, (NS, 16), 0) // 16 == lax.broadcasted_iota(jnp.int32, (NS, 16), 1))
        cols_of = (lax.broadcasted_iota(jnp.int32, (16, NS), 1) // 16 == lax.broadcasted_iota(jnp.int32, (16, NS), 0))
        rows_of, cols_of = rows_of.astype(F32).astype(BF16), cols_of.astype(F32).astype(BF16)

        def widen(pattern):
            return dot(dot(rows_of, pattern.astype(F32).astype(BF16)).astype(BF16), cols_of)

        source = lax.broadcasted_iota(jnp.int32, (NS, NS), 0)
        target = lax.broadcasted_iota(jnp.int32, (NS, NS), 1)
        place = (source // 8 % 2) * 128 + (source // 16) * 8 + source % 8
        order = (place == target).astype(F32).astype(BF16)
        high, low = split(first_ref[k] * widen(fpat_ref[k]))
        for part, dest in ((high, fh), (low, fl)):
            moved = dot(part, order).astype(BF16)
            for rh in (0, 1):
                dest[rh, :, k * 128 : (k + 1) * 128] = moved[:, rh * 128 : (rh + 1) * 128]
        high, low = split((second_ref[k] * widen(spat_ref[k])).T)
        zeros = jnp.zeros((64, NS), BF16)
        for cq in range(4):
            rows = slice(cq * 64, cq * 64 + 64)
            for third, part in enumerate((high[rows], low[rows], high[rows])):
                at = third * 128
                stc[k, cq, at : at + 64, :NS] = part
                stc[k, cq, at : at + 64, NS:] = zeros
                stc[k, cq, at + 64 : at + 128, :NS] = zeros
                stc[k, cq, at + 64 : at + 128, NS:] = part

    def select(q, first, last):
        if first == 1:
            part = gathered[q].at[pl.ds(0, GROUPS // 2 * PAIRS)]
            pltpu.make_async_copy(part, part, d2d_recv.at[q]).wait()

        def pick(j, dest, at):
            tiles = []
            for k in range(EVENTS):
                for u in range(OWN // 2):
                    even = sources_ref[k, group * MAC + j * OWN + 2 * u]
                    odd = sources_ref[k, group * MAC + j * OWN + 2 * u + 1]
                    one = pltpu.roll(gathered[q][lax.shift_right_logical(even, 1)], (even & 1) * 64, 1)
                    two = pltpu.roll(gathered[q][lax.shift_right_logical(odd, 1)], 64 - (odd & 1) * 64, 1)
                    tiles.append(jnp.where(low_lanes, one, two))
            for b, tile in enumerate(tiles):
                dest[at, b] = tile

        @pl.loop(first, last)
        def _(offset):
            j = sub_peer(offset)
            pick(j, outgo[q], j)
            pltpu.make_async_remote_copy(
                src_ref=outgo[q].at[j],
                dst_ref=income[q].at[piece],
                send_sem=xy_send.at[q],
                recv_sem=xy_recv.at[q],
                device_id=(group, j),
                device_id_type=MESH,
            ).start()

        if last == NSUB:
            pick(piece, income[q], piece)

    def stage1(q, events):
        rh, cq = q // 4, q % 4
        if events[0] == 0:
            part = income[q].at[pl.ds(0, NSUB - 1)]
            pltpu.make_async_copy(part, part, xy_recv.at[q]).wait()
        for k in events:
            block = income[q][:, k * OWN // 2 : (k + 1) * OWN // 2].reshape(NSUB * OWN // 2 * 8, 128)
            high, low = split(block)
            part = dot(jnp.concatenate([high, high, low], axis=1), stc[k, cq])
            if cq > 0:
                part = part + zacc[k]
            if cq < 3:
                zacc[k] = part
            else:
                for mm in range(OWN):
                    rate = rates_ref[k, piece * OWN + mm]
                    half = part[:, mm % 2 * NS : mm % 2 * NS + NS].reshape(NSUB, OWN // 2, 8, NS)
                    high, low = split(half[:, mm // 2].reshape(128, NS) * rate)
                    zh[mm, k * 128 : (k + 1) * 128, :] = high
                    zl[mm, k * 128 : (k + 1) * 128, :] = low

    def stage2(mm, rh):
        high, low = zh[mm], zl[mm]
        return dot(fh[rh], high) + dot(fh[rh], low) + dot(fl[rh], high)

    loads[0].wait()
    loads[1].wait()
    mass = stage(0, 0, jnp.zeros((8, 128), F32))
    pl.semaphore_wait(barrier, NSUB - 1 + GROUPS - 1)
    ring_start(0)
    mass = stage(0, 1, mass)

    def finish_stage(mass):
        mass = stage(1, 1, stage(1, 0, mass))
        sums[1:2, :] = jnp.sum(mass, axis=0, keepdims=True)
        for load in loads[2:]:
            load.wait()

    def first_product(mm):
        pacc[mm] = stage2(mm, 0)

    picks, products = [], [(0, functools.partial(prepare, k)) for k in range(EVENTS)]
    started = 1
    steps = sorted((q * STAGGER + t, q, t) for q in range(CHUNKS) for t in range(1, 5))
    for at, (now, q, t) in enumerate(steps):
        while started < CHUNKS and started * STAGGER <= now - 1:
            ring_start(started)
            started += 1
        ring_step(q, t)
        if at == 0:
            finish_stage(mass)
            continue
        for _ in range(BURST):
            for queue in (picks, products):
                if queue and queue[0][0] <= at:
                    queue.pop(0)[1]()
                    break
        if t == 4:
            picks.append((at + DELAY, functools.partial(select, q, 1, NSUB // 2)))
            picks.append((at + DELAY, functools.partial(select, q, NSUB // 2, NSUB)))
            products.append((at + DELAY + LAG, functools.partial(stage1, q, (0, 1))))
            products.append((at + DELAY + LAG, functools.partial(stage1, q, (2, 3))))
            if q == 3:
                products.extend((0, functools.partial(first_product, mm)) for mm in range(OWN))

    for _, task in picks + products:
        task()

    all_rows = lax.broadcasted_iota(jnp.int32, (NS, NS), 0)
    total = jnp.zeros((8, NS), F32)
    for mm in range(OWN):
        size = sizes_ref[group * MAC + piece * OWN + mm]
        product = jnp.where(all_rows < size, pacc[mm] + stage2(mm, 1), 0.0)
        total = total + jnp.sum(product.reshape(NS // 8, 8, NS), axis=0)
        pb[:, mm] = product.reshape(NSUB, 16, NS)
    sums[0:1, :] = jnp.sum(total[:, :128] + total[:, 128:], axis=0, keepdims=True)

    tsub[piece] = sums[...]

    @pl.loop(1, NSUB)
    def _(offset):
        pltpu.make_async_remote_copy(
            src_ref=sums,
            dst_ref=tsub.at[piece],
            send_sem=tot_send.at[0],
            recv_sem=tot_recv.at[0],
            device_id=(group, sub_peer(offset)),
            device_id_type=MESH,
        ).start()

    @pl.loop(1, NSUB)
    def _(offset):
        j = sub_peer(offset)
        pltpu.make_async_remote_copy(
            src_ref=pb.at[j],
            dst_ref=out_ref.at[piece],
            send_sem=out_send,
            recv_sem=out_recv,
            device_id=(group, j),
            device_id_type=MESH,
        ).start()

    out_ref[piece] = pb[piece]
    pltpu.make_async_copy(tsub.at[pl.ds(0, NSUB - 1)], tsub.at[pl.ds(0, NSUB - 1)], tot_recv.at[0]).wait()
    tgrp[group] = jnp.sum(tsub[...], axis=0)

    @pl.loop(1, GROUPS)
    def _(offset):
        pltpu.make_async_remote_copy(
            src_ref=tgrp.at[group],
            dst_ref=tgrp.at[group],
            send_sem=tot_send.at[1],
            recv_sem=tot_recv.at[1],
            device_id=((group + offset) % GROUPS, piece),
            device_id_type=MESH,
        ).start()

    for q in range(CHUNKS):
        part = gathered[q].at[pl.ds(0, 14 * HALF)]
        pltpu.make_async_copy(part, part, ring_send.at[q]).wait()
        part = gathered[q].at[pl.ds(0, PAIRS + 14 * HALF)]
        pltpu.make_async_copy(part, part, d2d_send.at[q]).wait()
        part = outgo[q].at[pl.ds(0, NSUB - 1)]
        pltpu.make_async_copy(part, part, xy_send.at[q]).wait()
    part = tsub.at[pl.ds(0, NSUB - 1)]
    pltpu.make_async_copy(part, part, tot_send.at[0]).wait()
    live = jnp.sum(sizes_vec_ref[...].astype(F32)) * NS

    part = tgrp.at[pl.ds(0, GROUPS - 1)]
    pltpu.make_async_copy(part, part, tot_recv.at[1]).wait()
    both = jnp.sum(tgrp[...], axis=0)
    total, mass = jnp.sum(both[0:1]), jnp.sum(both[1:2])
    pick = lax.broadcasted_iota(jnp.int32, (8, 128), 0) == 0
    numer = jnp.where(pick, jnp.full((8, 128), live, F32), jnp.full((8, 128), total, F32))
    denom = jnp.where(pick, jnp.full((8, 128), total, F32), jnp.full((8, 128), mass, F32))
    stats_ref[...] = numer / denom

    pltpu.make_async_copy(part, part, tot_send.at[1]).wait()
    part = pb.at[pl.ds(0, NSUB - 1)]
    pltpu.make_async_copy(part, part, out_recv).wait()
    pltpu.make_async_copy(part, part, out_send).wait()


def rescale(product_ref, stats_ref, scaled_ref, growth_ref):
    scaled_ref[...] = product_ref[...] * stats_ref[0:1, 0:1].reshape(1, 1, 1)
    growth_ref[...] = stats_ref[1:2, 0:1]


def on_device(
    macro_state, macro_sizes, block_sources, event_rates, first_factor, first_pattern, second_factor, second_pattern
):
    vmem, hbm = pl.BlockSpec(memory_space=pltpu.VMEM), pl.BlockSpec(memory_space=pltpu.HBM)
    dma = pltpu.SemaphoreType.DMA
    product, stats = pl.pallas_call(
        kernel,
        out_shape=(
            pltpu.VMEM((NSUB, OWN, 16, NS), F32),
            pltpu.VMEM((8, 128), F32),
        ),
        in_specs=[hbm, hbm, vmem, hbm, hbm, hbm, hbm, hbm, hbm],
        out_specs=(vmem, vmem),
        scratch_shapes=[pltpu.VMEM((GROUPS * PAIRS, 8, 128), F32) for _ in range(CHUNKS)]
        + [pltpu.VMEM((NSUB, BLK // 2, 8, 128), F32) for _ in range(2 * CHUNKS)]
        + [
            pltpu.VMEM((MAC, 16, NS), F32),
            pltpu.SMEM((GROUPS * MAC,), jnp.int32),
            pltpu.SMEM((EVENTS, GROUPS * MAC), jnp.int32),
            pltpu.SMEM((EVENTS, MAC), F32),
            pltpu.VMEM((EVENTS, NS, NS), F32),
            pltpu.VMEM((EVENTS, 16, 16), jnp.int32),
            pltpu.VMEM((EVENTS, NS, NS), F32),
            pltpu.VMEM((EVENTS, 16, 16), jnp.int32),
            pltpu.VMEM((2, NS, EVENTS * 128), BF16),
            pltpu.VMEM((2, NS, EVENTS * 128), BF16),
            pltpu.VMEM((EVENTS, 4, 384, 2 * NS), BF16),
            pltpu.VMEM((EVENTS, NSUB * OWN // 2 * 8, 2 * NS), F32),
            pltpu.VMEM((OWN, EVENTS * 128, NS), BF16),
            pltpu.VMEM((OWN, EVENTS * 128, NS), BF16),
            pltpu.VMEM((OWN, NS, NS), F32),
            pltpu.VMEM((NSUB, OWN, 16, NS), F32),
            pltpu.VMEM((2, 128), F32),
            pltpu.VMEM((NSUB, 2, 128), F32),
            pltpu.VMEM((GROUPS, 2, 128), F32),
            dma((8,)),
            dma((CHUNKS,)),
            dma((CHUNKS * 16,)),
            dma((CHUNKS,)),
            dma((CHUNKS,)),
            dma((CHUNKS,)),
            dma((CHUNKS,)),
            dma((2,)),
            dma((2,)),
            dma,
            dma,
        ],
        compiler_params=pltpu.CompilerParams(
            collective_id=0, has_side_effects=True, vmem_limit_bytes=56 * 1024 * 1024
        ),
    )(
        macro_state,
        macro_sizes,
        macro_sizes.reshape(8, 128),
        block_sources.T,
        event_rates.T,
        first_factor,
        first_pattern,
        second_factor,
        second_pattern,
    )
    scaled, growth = pl.pallas_call(
        rescale,
        out_shape=(
            jax.ShapeDtypeStruct((MAC, 16, NS), F32),
            jax.ShapeDtypeStruct((1, 1), F32),
        ),
        in_specs=[vmem, vmem],
        out_specs=(vmem, vmem),
    )(
        pltpu.with_memory_space_constraint(product.reshape(MAC, 16, NS), pltpu.VMEM),
        pltpu.with_memory_space_constraint(stats, pltpu.VMEM),
    )
    return scaled, growth.reshape(())


def solution(mesh):
    return jax.shard_map(
        on_device,
        mesh=mesh,
        in_specs=(P("grp", "sub", None), P(), P(), P("grp", None), P(), P(), P(), P()),
        out_specs=(P("grp", "sub", None), P()),
        check_vma=False,
    )
```

```python
import functools

import jax
import jax.numpy as jnp
from jax import lax
from jax.experimental import pallas as pl
from jax.experimental.pallas import tpu as pltpu
from jax.sharding import PartitionSpec as P

MESH = pl.DeviceIdType.MESH
F32, BF16 = jnp.float32, jnp.bfloat16
NS = 256
EVENTS = 4
NZ = 8
NSUB = 16
MAC = 64
OWN = MAC // NSUB
BLK = OWN * EVENTS
GROUPS = 2 * NZ
PAIRS = MAC // 2
HALF = PAIRS // 2
CHUNKS = 8
DELAY = 2
LAG = 6
BURST = 1
STAGGER = 1.0
CW, CCW = 0, 1


def split(x):
    high = x.astype(BF16)
    return high, (x - high.astype(F32)).astype(BF16)


def dot(a, b):
    return jnp.dot(a, b, preferred_element_type=F32)


def kernel(
    state_hbm, sizes_hbm, sizes_vec_ref, sources_hbm, rates_hbm, first_hbm, fpat_hbm, second_hbm, spat_hbm,
    out_ref, stats_ref,
    *scratch,
):
    gathered, outgo, income = scratch[:CHUNKS], scratch[CHUNKS : 2 * CHUNKS], scratch[2 * CHUNKS : 3 * CHUNKS]
    (
        state_ref, sizes_ref, sources_ref, rates_ref, first_ref, fpat_ref, second_ref, spat_ref,
        fh, fl, stc, zacc, zh, zl, pacc, pb, sums, tsub, tgrp,
        load_sem, ring_send, ring_recv, d2d_send, d2d_recv, xy_send, xy_recv, tot_send, tot_recv, out_send, out_recv,
    ) = scratch[3 * CHUNKS :]
    group, piece = lax.axis_index("grp"), lax.axis_index("sub")
    z, core = group // 2, group % 2
    y, x = piece // 4, piece % 4
    sibling = z * 2 + (1 - core)

    def ring_group(distance):
        return ((z + distance + NZ) % NZ) * 2 + core

    def sub_peer(offset):
        return ((y + offset // 4) % 4) * 4 + (x + offset % 4) % 4

    barrier = pltpu.get_barrier_semaphore()

    @pl.loop(1, GROUPS)
    def _(offset):
        pl.semaphore_signal(barrier, inc=1, device_id=((group + offset) % GROUPS, piece), device_id_type=MESH)

    @pl.loop(1, NSUB)
    def _(offset):
        pl.semaphore_signal(barrier, inc=1, device_id=(group, sub_peer(offset)), device_id_type=MESH)

    loads = [
        pltpu.make_async_copy(source, dest, load_sem.at[i])
        for i, (source, dest) in enumerate(
            (
                (state_hbm, state_ref),
                (sizes_hbm, sizes_ref),
                (sources_hbm, sources_ref),
                (rates_hbm, rates_ref),
                (first_hbm, first_ref),
                (fpat_hbm, fpat_ref),
                (second_hbm, second_ref),
                (spat_hbm, spat_ref),
            )
        )
    ]
    for load in loads:
        load.start()

    row_iota = lax.broadcasted_iota(jnp.int32, (8, 128), 0)
    low_lanes = lax.broadcasted_iota(jnp.int32, (8, 128), 1) < 64

    def stage(rh, ch, mass):
        rows = row_iota + (piece * 16 + rh * 8)
        q = rh * 4 + ch * 2

        def masked(m):
            tile = state_ref[m, pl.ds(8 * rh, 8), pl.ds(128 * ch, 128)]
            return jnp.where(rows < sizes_ref[group * MAC + m], tile, 0.0)

        def body(p, mass):
            even, odd = masked(2 * p), masked(2 * p + 1)
            gathered[q][group * PAIRS + p] = jnp.where(low_lanes, even, pltpu.roll(odd, 64, 1))
            gathered[q + 1][group * PAIRS + p] = jnp.where(low_lanes, pltpu.roll(even, 64, 1), odd)
            return mass + even + odd

        return lax.fori_loop(0, PAIRS, body, mass, unroll=8)

    def ring_piece(q, distance, h):
        return gathered[q].at[pl.ds(ring_group(distance) * PAIRS + HALF * h, HALF)]

    def ring_copy(q, way, t, h):
        sign = -1 if way == CW else 1
        part = ring_piece(q, sign * (t - 1), h)
        return pltpu.make_async_remote_copy(
            src_ref=part,
            dst_ref=part,
            send_sem=ring_send.at[q],
            recv_sem=ring_recv.at[((q * 2 + way) * 4 + t - 1) * 2 + h],
            device_id=(ring_group(-sign), piece),
            device_id_type=MESH,
        )

    def ring_wait(q, way, t, h):
        sign = -1 if way == CW else 1
        part = ring_piece(q, sign * t, h)
        pltpu.make_async_copy(part, part, ring_recv.at[((q * 2 + way) * 4 + t - 1) * 2 + h]).wait()

    def sibling_copy(q, part):
        pltpu.make_async_remote_copy(
            src_ref=part,
            dst_ref=part,
            send_sem=d2d_send.at[q],
            recv_sem=d2d_recv.at[q],
            device_id=(sibling, piece),
            device_id_type=MESH,
        ).start()

    def carried(way, t):
        return (0, 1) if t < 4 else ((0,) if way == CW else (1,))

    def ring_start(q):
        for h in (0, 1):
            for way in (CW, CCW):
                ring_copy(q, way, 1, h).start()
        sibling_copy(q, gathered[q].at[pl.ds(group * PAIRS, PAIRS)])

    def ring_step(q, t):
        for h in (0, 1):
            for way in (CW, CCW):
                if h in carried(way, t):
                    ring_wait(q, way, t, h)
                    if t < 4 and h in carried(way, t + 1):
                        ring_copy(q, way, t + 1, h).start()
                    if t == 4:
                        sibling_copy(q, ring_piece(q, -t if way == CW else t, h))
                    elif h == 1:
                        sibling_copy(q, gathered[q].at[pl.ds(ring_group(-t if way == CW else t) * PAIRS, PAIRS)])

    def prepare(k):
        rows_of = (lax.broadcasted_iota(jnp.int32, (NS, 16), 0) // 16 == lax.broadcasted_iota(jnp.int32, (NS, 16), 1))
        cols_of = (lax.broadcasted_iota(jnp.int32, (16, NS), 1) // 16 == lax.broadcasted_iota(jnp.int32, (16, NS), 0))
        rows_of, cols_of = rows_of.astype(F32).astype(BF16), cols_of.astype(F32).astype(BF16)

        def widen(pattern):
            return dot(dot(rows_of, pattern.astype(F32).astype(BF16)).astype(BF16), cols_of)

        source = lax.broadcasted_iota(jnp.int32, (NS, NS), 0)
        target = lax.broadcasted_iota(jnp.int32, (NS, NS), 1)
        place = (source // 8 % 2) * 128 + (source // 16) * 8 + source % 8
        order = (place == target).astype(F32).astype(BF16)
        high, low = split(first_ref[k] * widen(fpat_ref[k]))
        for part, dest in ((high, fh), (low, fl)):
            moved = dot(part, order).astype(BF16)
            for rh in (0, 1):
                dest[rh, :, k * 128 : (k + 1) * 128] = moved[:, rh * 128 : (rh + 1) * 128]
        high, low = split((second_ref[k] * widen(spat_ref[k])).T)
        zeros = jnp.zeros((64, NS), BF16)
        for cq in range(4):
            rows = slice(cq * 64, cq * 64 + 64)
            for third, part in enumerate((high[rows], low[rows], high[rows])):
                at = third * 128
                stc[k, cq, at : at + 64, :NS] = part
                stc[k, cq, at : at + 64, NS:] = zeros
                stc[k, cq, at + 64 : at + 128, :NS] = zeros
                stc[k, cq, at + 64 : at + 128, NS:] = part

    def select(q, first, last):
        if first == 1:
            part = gathered[q].at[pl.ds(0, GROUPS // 2 * PAIRS)]
            pltpu.make_async_copy(part, part, d2d_recv.at[q]).wait()

        def pick(j, dest, at):
            tiles = []
            for k in range(EVENTS):
                for u in range(OWN // 2):
                    even = sources_ref[k, group * MAC + j * OWN + 2 * u]
                    odd = sources_ref[k, group * MAC + j * OWN + 2 * u + 1]
                    one = pltpu.roll(gathered[q][lax.shift_right_logical(even, 1)], (even & 1) * 64, 1)
                    two = pltpu.roll(gathered[q][lax.shift_right_logical(odd, 1)], 64 - (odd & 1) * 64, 1)
                    tiles.append(jnp.where(low_lanes, one, two))
            for b, tile in enumerate(tiles):
                dest[at, b] = tile

        @pl.loop(first, last)
        def _(offset):
            j = sub_peer(offset)
            pick(j, outgo[q], j)
            pltpu.make_async_remote_copy(
                src_ref=outgo[q].at[j],
                dst_ref=income[q].at[piece],
                send_sem=xy_send.at[q],
                recv_sem=xy_recv.at[q],
                device_id=(group, j),
                device_id_type=MESH,
            ).start()

        if last == NSUB:
            pick(piece, income[q], piece)

    def stage1(q, events):
        rh, cq = q // 4, q % 4
        if events[0] == 0:
            part = income[q].at[pl.ds(0, NSUB - 1)]
            pltpu.make_async_copy(part, part, xy_recv.at[q]).wait()
        for k in events:
            block = income[q][:, k * OWN // 2 : (k + 1) * OWN // 2].reshape(NSUB * OWN // 2 * 8, 128)
            high, low = split(block)
            part = dot(jnp.concatenate([high, high, low], axis=1), stc[k, cq])
            if cq > 0:
                part = part + zacc[k]
            if cq < 3:
                zacc[k] = part
            else:
                for mm in range(OWN):
                    rate = rates_ref[k, piece * OWN + mm]
                    half = part[:, mm % 2 * NS : mm % 2 * NS + NS].reshape(NSUB, OWN // 2, 8, NS)
                    high, low = split(half[:, mm // 2].reshape(128, NS) * rate)
                    zh[mm, k * 128 : (k + 1) * 128, :] = high
                    zl[mm, k * 128 : (k + 1) * 128, :] = low

    def stage2(mm, rh):
        high, low = zh[mm], zl[mm]
        return dot(fh[rh], high) + dot(fh[rh], low) + dot(fl[rh], high)

    loads[0].wait()
    loads[1].wait()
    mass = stage(0, 0, jnp.zeros((8, 128), F32))
    pl.semaphore_wait(barrier, NSUB - 1 + GROUPS - 1)
    ring_start(0)
    mass = stage(0, 1, mass)

    def finish_stage(mass):
        mass = stage(1, 1, stage(1, 0, mass))
        sums[1:2, :] = jnp.sum(mass, axis=0, keepdims=True)
        for load in loads[2:]:
            load.wait()

    def first_product(mm):
        pacc[mm] = stage2(mm, 0)

    picks, products = [], [(0, functools.partial(prepare, k)) for k in range(EVENTS)]
    started = 1
    steps = sorted((q * STAGGER + t, q, t) for q in range(CHUNKS) for t in range(1, 5))
    for at, (now, q, t) in enumerate(steps):
        while started < CHUNKS and started * STAGGER <= now - 1:
            ring_start(started)
            started += 1
        ring_step(q, t)
        if at == 0:
            finish_stage(mass)
            continue
        for _ in range(BURST):
            for queue in (picks, products):
                if queue and queue[0][0] <= at:
                    queue.pop(0)[1]()
                    break
        if t == 4:
            picks.append((at + DELAY, functools.partial(select, q, 1, NSUB // 2)))
            picks.append((at + DELAY, functools.partial(select, q, NSUB // 2, NSUB)))
            products.append((at + DELAY + LAG, functools.partial(stage1, q, (0, 1))))
            products.append((at + DELAY + LAG, functools.partial(stage1, q, (2, 3))))
            if q == 3:
                products.extend((0, functools.partial(first_product, mm)) for mm in range(OWN))

    for _, task in picks + products:
        task()

    all_rows = lax.broadcasted_iota(jnp.int32, (NS, NS), 0)
    total = jnp.zeros((8, NS), F32)
    for mm in range(OWN):
        size = sizes_ref[group * MAC + piece * OWN + mm]
        product = jnp.where(all_rows < size, pacc[mm] + stage2(mm, 1), 0.0)
        total = total + jnp.sum(product.reshape(NS // 8, 8, NS), axis=0)
        pb[:, mm] = product.reshape(NSUB, 16, NS)
    sums[0:1, :] = jnp.sum(total[:, :128] + total[:, 128:], axis=0, keepdims=True)

    tsub[piece] = sums[...]

    @pl.loop(1, NSUB)
    def _(offset):
        pltpu.make_async_remote_copy(
            src_ref=sums,
            dst_ref=tsub.at[piece],
            send_sem=tot_send.at[0],
            recv_sem=tot_recv.at[0],
            device_id=(group, sub_peer(offset)),
            device_id_type=MESH,
        ).start()

    @pl.loop(1, NSUB)
    def _(offset):
        j = sub_peer(offset)
        pltpu.make_async_remote_copy(
            src_ref=pb.at[j],
            dst_ref=out_ref.at[piece],
            send_sem=out_send,
            recv_sem=out_recv,
            device_id=(group, j),
            device_id_type=MESH,
        ).start()

    out_ref[piece] = pb[piece]
    pltpu.make_async_copy(tsub.at[pl.ds(0, NSUB - 1)], tsub.at[pl.ds(0, NSUB - 1)], tot_recv.at[0]).wait()
    tgrp[group] = jnp.sum(tsub[...], axis=0)

    @pl.loop(1, GROUPS)
    def _(offset):
        pltpu.make_async_remote_copy(
            src_ref=tgrp.at[group],
            dst_ref=tgrp.at[group],
            send_sem=tot_send.at[1],
            recv_sem=tot_recv.at[1],
            device_id=((group + offset) % GROUPS, piece),
            device_id_type=MESH,
        ).start()

    for q in range(CHUNKS):
        part = gathered[q].at[pl.ds(0, 14 * HALF)]
        pltpu.make_async_copy(part, part, ring_send.at[q]).wait()
        part = gathered[q].at[pl.ds(0, PAIRS + 14 * HALF)]
        pltpu.make_async_copy(part, part, d2d_send.at[q]).wait()
        part = outgo[q].at[pl.ds(0, NSUB - 1)]
        pltpu.make_async_copy(part, part, xy_send.at[q]).wait()
    part = tsub.at[pl.ds(0, NSUB - 1)]
    pltpu.make_async_copy(part, part, tot_send.at[0]).wait()
    live = jnp.sum(sizes_vec_ref[...].astype(F32)) * NS

    part = tgrp.at[pl.ds(0, GROUPS - 1)]
    pltpu.make_async_copy(part, part, tot_recv.at[1]).wait()
    both = jnp.sum(tgrp[...], axis=0)
    total, mass = jnp.sum(both[0:1]), jnp.sum(both[1:2])
    pick = lax.broadcasted_iota(jnp.int32, (8, 128), 0) == 0
    numer = jnp.where(pick, jnp.full((8, 128), live, F32), jnp.full((8, 128), total, F32))
    denom = jnp.where(pick, jnp.full((8, 128), total, F32), jnp.full((8, 128), mass, F32))
    stats_ref[...] = numer / denom

    pltpu.make_async_copy(part, part, tot_send.at[1]).wait()
    part = pb.at[pl.ds(0, NSUB - 1)]
    pltpu.make_async_copy(part, part, out_recv).wait()
    pltpu.make_async_copy(part, part, out_send).wait()


def rescale(product_ref, stats_ref, scaled_ref, growth_ref):
    scaled_ref[...] = product_ref[...] * stats_ref[0:1, 0:1].reshape(1, 1, 1)
    growth_ref[...] = stats_ref[1:2, 0:1]


def on_device(
    macro_state, macro_sizes, block_sources, event_rates, first_factor, first_pattern, second_factor, second_pattern
):
    vmem, hbm = pl.BlockSpec(memory_space=pltpu.VMEM), pl.BlockSpec(memory_space=pltpu.HBM)
    dma = pltpu.SemaphoreType.DMA
    product, stats = pl.pallas_call(
        kernel,
        out_shape=(
            pltpu.VMEM((NSUB, OWN, 16, NS), F32),
            pltpu.VMEM((8, 128), F32),
        ),
        in_specs=[hbm, hbm, vmem, hbm, hbm, hbm, hbm, hbm, hbm],
        out_specs=(vmem, vmem),
        scratch_shapes=[pltpu.VMEM((GROUPS * PAIRS, 8, 128), F32) for _ in range(CHUNKS)]
        + [pltpu.VMEM((NSUB, BLK // 2, 8, 128), F32) for _ in range(2 * CHUNKS)]
        + [
            pltpu.VMEM((MAC, 16, NS), F32),
            pltpu.SMEM((GROUPS * MAC,), jnp.int32),
            pltpu.SMEM((EVENTS, GROUPS * MAC), jnp.int32),
            pltpu.SMEM((EVENTS, MAC), F32),
            pltpu.VMEM((EVENTS, NS, NS), F32),
            pltpu.VMEM((EVENTS, 16, 16), jnp.int32),
            pltpu.VMEM((EVENTS, NS, NS), F32),
            pltpu.VMEM((EVENTS, 16, 16), jnp.int32),
            pltpu.VMEM((2, NS, EVENTS * 128), BF16),
            pltpu.VMEM((2, NS, EVENTS * 128), BF16),
            pltpu.VMEM((EVENTS, 4, 384, 2 * NS), BF16),
            pltpu.VMEM((EVENTS, NSUB * OWN // 2 * 8, 2 * NS), F32),
            pltpu.VMEM((OWN, EVENTS * 128, NS), BF16),
            pltpu.VMEM((OWN, EVENTS * 128, NS), BF16),
            pltpu.VMEM((OWN, NS, NS), F32),
            pltpu.VMEM((NSUB, OWN, 16, NS), F32),
            pltpu.VMEM((2, 128), F32),
            pltpu.VMEM((NSUB, 2, 128), F32),
            pltpu.VMEM((GROUPS, 2, 128), F32),
            dma((8,)),
            dma((CHUNKS,)),
            dma((CHUNKS * 16,)),
            dma((CHUNKS,)),
            dma((CHUNKS,)),
            dma((CHUNKS,)),
            dma((CHUNKS,)),
            dma((2,)),
            dma((2,)),
            dma,
            dma,
        ],
        compiler_params=pltpu.CompilerParams(
            collective_id=0, has_side_effects=True, vmem_limit_bytes=56 * 1024 * 1024
        ),
    )(
        macro_state,
        macro_sizes,
        macro_sizes.reshape(8, 128),
        block_sources.T,
        event_rates.T,
        first_factor,
        first_pattern,
        second_factor,
        second_pattern,
    )
    scaled, growth = pl.pallas_call(
        rescale,
        out_shape=(
            jax.ShapeDtypeStruct((MAC, 16, NS), F32),
            jax.ShapeDtypeStruct((1, 1), F32),
        ),
        in_specs=[vmem, vmem],
        out_specs=(vmem, vmem),
    )(
        pltpu.with_memory_space_constraint(product.reshape(MAC, 16, NS), pltpu.VMEM),
        pltpu.with_memory_space_constraint(stats, pltpu.VMEM),
    )
    return scaled, growth.reshape(())


def solution(mesh):
    return jax.shard_map(
        on_device,
        mesh=mesh,
        in_specs=(P("grp", "sub", None), P(), P(), P("grp", None), P(), P(), P(), P()),
        out_specs=(P("grp", "sub", None), P()),
        check_vma=False,
    )
```
